256 devices in a mesh: dp: 16 (over y, z_hi, core), grp: 16 (over x, z_lo).
Axes of the slice: x: 4, y: 4, z: 8 (z_hi: 2, z_lo: 4; z = z_hi * 4 + z_lo), core: 2. Of those that a mesh axis runs over, the one named last changes fastest.
Arguments:
- partial_grads: bfloat16 [16, 192, 512, 512], P('dp', None, 'grp'), may hold values from -6 to 6
- owners: int32 [16, 12, 1], P('dp'), may hold values from 0 to 15; in each aligned block of 12 rows (0 to 11, 12 to 23, ..., all dimensions but the last counted through in order) at most 2 rows name the same one
- prev_stats: float32 [16, 16, 2, 2, 512, 512], P('dp', 'grp'), may hold values from -8 to 61440, as said below
Outputs:
- directions: float32 [192, 512, 512], P('dp', 'grp')
The draws below stay inside these ranges and needn't reach their ends.
Inputs may be any that keep to these rules, and one draw needn't show every extreme that they name: `owners`: among the 12 blocks of one dp index no owner appears more than 2 times. `prev_stats`: each slot holds two symmetric positive definite matrices.
All inputs are finite; a program needn't handle non-finite values.
Results may differ from the reference program's by a relative error of at most 0.0029.
Values may be sent and summed in bfloat16 or wider, within the bound.
No kernel may reach another device: no remote copies, remote signals or barrier semaphores. Data moves between devices by JAX's collectives and lax.ppermute only.
A program may use at most 128 MiB of HBM per device.

```python
import math
import jax
import jax.numpy as jnp
import numpy as np
from jax import lax

BS = 512
BPD = 12
CAP = 2
ITERS = 2
NB = 192
N_DP = 16
N_GRP = 16


def draw_prev_stats(key, part):
    key = jax.random.fold_in(key, 7)
    key_off, key_diag = jax.random.split(key)
    shape = (N_DP, N_GRP, CAP, 2, BS, BS)
    offdiag = jax.random.uniform(key_off, shape, jnp.float32, -1.0, 1.0)
    symmetric = 0.5 * (offdiag + jnp.swapaxes(offdiag, -1, -2))
    lowest, highest = (1.5, 15.0)
    logs = jax.random.uniform(key_diag, shape[:-1], jnp.float32, jnp.log(lowest), jnp.log(highest))
    diag_scale = jnp.exp(logs)
    identity = jnp.eye(BS, dtype=jnp.float32)
    return 8.0 * symmetric * (1.0 - identity) + identity * (8.0 * BS) * diag_scale[..., None]


def strengthened(drawn, rng, source, target, shards_of, factor):
    owner, partner = [(jnp.arange(drawn.shape[axis_at]) // (drawn.shape[axis_at] // shards_of)).reshape([-1 if axis == axis_at else 1 for axis in range(drawn.ndim)]) for axis_at in (source, target)]
    chosen = jax.random.permutation(rng, shards_of)[partner]
    strong = (owner == chosen) | (owner == (partner + shards_of // 2) % shards_of)
    return jnp.where(strong, factor * drawn, drawn)


def block_scale(own_key, shape, cuts, smallest, high):
    gain = 1.0
    for dim, shards_of in cuts:
        draws = jax.random.uniform(jax.random.fold_in(jax.random.fold_in(own_key, 6), dim), (shards_of,), jnp.float32, smallest / len(cuts), high / len(cuts))
        gain = gain * jnp.repeat(jnp.exp(draws), shape[dim] // shards_of).reshape((-1,) + (1,) * (len(shape) - 1 - dim))
    return gain


def shared_out(stream_key, own, number, rows, count, top, most, lean):
    ranking = jax.random.permutation(stream_key, count)
    crowded, usual = shares(count, rows * top, most, lean, True), shares(count, rows * top, most, lean, False)
    places = jnp.arange(count)

    def named(lengths, turn):
        used = int((lengths > 0).sum())
        fixed = max(1, used // 4)
        passed = fixed + (places - fixed + turn * (used - fixed)) % max(1, count - fixed)
        return jnp.zeros((count,), jnp.int32).at[ranking[jnp.where(places < fixed, places, passed)]].set(jnp.asarray(lengths, jnp.int32))

    lengths = jnp.where(number % 4 == 0, named(crowded, number // 4), named(usual, number - number // 4 - 1))
    mixed = jax.random.permutation(jax.random.fold_in(own, 3), count)
    source_of, taker = mixed[0:count // 2 * 2:2], mixed[1:count // 2 * 2:2]
    margin = jnp.minimum(lengths[source_of] - 1, most - lengths[taker]) // 2
    margin = jnp.where((source_of == ranking[0]) | (taker == ranking[0]) | (lengths[taker] == 0), 0, jnp.maximum(margin, 0))
    passed = jax.random.randint(jax.random.fold_in(own, 4), (count // 2,), 0, 1 << 20) % (margin + 1)
    lengths = lengths.at[source_of].add(-passed).at[taker].add(passed)
    items = jnp.searchsorted(jnp.cumsum(lengths), jnp.arange(rows * top), side="right").astype(jnp.int32)
    table = items.reshape(top, rows).T
    table = table[jax.random.permutation(jax.random.fold_in(own, 1), rows)]
    turn = jax.random.randint(jax.random.fold_in(own, 2), (rows, 1), 0, top)
    return jnp.take_along_axis(table, (jnp.arange(top)[None, :] + turn) % top, axis=1)


def shares(count, total, limit, skew, full):
    portions = [(1 << 20) // math.isqrt(rank ** skew) + 1 for rank in range(1, count + 1)]
    largest = limit if full else min(limit, max(-(-total // count), total * portions[0] // sum(portions)))
    least = 1 if total - largest >= count - 1 else 0
    given, surplus = [largest] + [least] * (count - 1), total - largest - least * (count - 1)
    while surplus > 0:
        movable = [i for i in range(1, count) if given[i] < largest] or [i for i in range(1, count) if given[i] < limit]
        whole, budget = sum([portions[i] for i in movable]), surplus
        for i in movable:
            extra = min(limit - given[i], max(1, budget * portions[i] // whole), surplus)
            given[i] = given[i] + extra
            surplus = surplus - extra
    return np.array(given)


def bell_draw_with(own_key, shape, scale, limit, cuts, heavy, kind=jnp.bfloat16):
    entries = scale * jax.random.normal(own_key, shape, jnp.float32)
    if cuts:
        entries = entries * block_scale(own_key, shape, cuts, -0.22, 0.18)
    return jnp.clip(strengthened(entries, jax.random.fold_in(own_key, 3), *heavy), -limit, limit).astype(kind)


def setup_inputs(seed: int = 0) -> dict:
    key_of = jax.random.split(jax.random.key(seed), 4)
    partial_grads = bell_draw_with(key_of[0], (N_DP, NB, BS, BS), 1.0, 6.0, ((0, 16), (2, 16)), (0, 1, 16, 2.0))
    owners_keys = jax.random.split(jax.random.fold_in(key_of[1], 1), N_DP * BPD // BPD)
    owners_turns = jax.random.permutation(jax.random.fold_in(key_of[1], 3), N_DP * BPD // BPD)
    owners = jax.vmap(lambda own, number: shared_out(jax.random.fold_in(key_of[1], 2), own, number, BPD, N_GRP, 1, CAP, 2))(owners_keys, owners_turns).reshape((N_DP, BPD, 1))
    prev_stats = draw_prev_stats(jax.random.fold_in(key_of[3], 71), 0)
    return dict(partial_grads=partial_grads, owners=owners, prev_stats=prev_stats)


def matmul_high(left_side, right_side):
    return jnp.matmul(left_side, right_side, precision=lax.Precision.HIGHEST)

def inverse_root(stats):
    width = stats.shape[-1]
    identity = jnp.eye(width, dtype=jnp.float32)
    frobenius = width * jnp.sqrt(lax.optimization_barrier(jnp.mean(stats * stats, axis=(-2, -1), keepdims=True)) + 1e-06)
    matrix = (stats / frobenius + 0.1 * identity) / 1.1
    root = identity
    for step in range(ITERS):
        factor = (5.0 * identity - matrix) * 0.25
        if step == 0:
            root = factor * 1.1 ** (-0.25)
        else:
            root = matmul_high(root, factor)
        if step + 1 < ITERS:
            square = matmul_high(factor, factor)
            fourth = matmul_high(square, square)
            matrix = matmul_high(fourth, matrix)
    return root

def direction_of(grad_block, stats_pair):
    wide = grad_block.astype(jnp.float32)
    left_gram = matmul_high(wide, wide.T)
    right_gram = matmul_high(wide.T, wide)
    grams = jnp.stack([left_gram, right_gram], axis=0)
    roots = inverse_root(0.5 * stats_pair + 0.5 * grams)
    precond = matmul_high(matmul_high(roots[0], wide), roots[1])
    scale = jnp.sqrt(jnp.mean(wide * wide)) / jnp.sqrt(jnp.mean(precond * precond) + 1e-06)
    return precond * scale

def reference(partial_grads, owners, prev_stats):
    owner_table = owners[:, :, 0].astype(jnp.int32)
    count = owner_table.shape[1]
    same = owner_table[:, :, None] == owner_table[:, None, :]
    before = jnp.arange(count)[None, :] < jnp.arange(count)[:, None]
    slots = lax.optimization_barrier(jnp.sum(jnp.where(same & before[None], 1, 0), axis=2)).astype(jnp.int32)

    def one_block(index):
        row = (index // count).astype(jnp.int32)
        place = (index % count).astype(jnp.int32)
        pieces = lax.dynamic_index_in_dim(partial_grads, index, 1, keepdims=False)
        grad_block = lax.optimization_barrier(jnp.sum(pieces.astype(jnp.float32), axis=0)).astype(jnp.bfloat16)
        owner = owner_table[row, place]
        slot = slots[row, place]
        stats_pair = prev_stats[row, owner, slot]
        return direction_of(grad_block, stats_pair)
    return lax.map(one_block, jnp.arange(NB).astype(jnp.int32))
```

```python
from math import comb

import jax
import jax.numpy as jnp
from jax import lax
from jax.experimental import pallas as pl
from jax.experimental.pallas import tpu as pltpu
from jax.sharding import PartitionSpec as P

NY, NZ, NC = 4, 2, 2
SCALE = 1024.0
MIB = 1024 * 1024


def dp_perm(dy=0, dz=0, dc=0):
    pairs = []
    for y in range(NY):
        for z in range(NZ):
            for c in range(NC):
                source = (y * NZ + z) * NC + c
                target = (((y + dy) % NY) * NZ + (z + dz) % NZ) * NC + (c + dc) % NC
                pairs.append((source, target))
    return pairs


CORE = dp_perm(dc=1)
ZHI = dp_perm(dz=1)
UP = dp_perm(dy=1)
DOWN = dp_perm(dy=-1)


def root_coefficients():
    f0, f1 = 27.0 / 22.0, -5.0 / 22.0
    fifth = [comb(5, i) * f0 ** (5 - i) * f1**i for i in range(6)]
    product = [0.0] * 7
    for i, value in enumerate(fifth):
        product[i] += value / 11.0
        product[i + 1] += value * 10.0 / 11.0
    coefs = [-value / 4.0 for value in product]
    coefs[0] += 5.0 * f0 / 4.0
    coefs[1] += 5.0 * f1 / 4.0
    return [value * 1.1 ** (-0.25) for value in coefs]


COEF = root_coefficients()


def dot(a, b, dims=((1,), (0,))):
    return lax.dot_general(a, b, (dims, ((), ())), preferred_element_type=jnp.float32)


def root_rest(stats):
    width = stats.shape[-1]
    mean = jnp.sum(stats * stats, axis=(0, 1), keepdims=True) * (1.0 / (width * width))
    b1 = stats * (1.0 / (width * jnp.sqrt(mean + 1e-06)))
    b1h = b1.astype(jnp.bfloat16)
    b2 = dot(b1h, b1h)
    b2h = b2.astype(jnp.bfloat16)
    b3 = dot(b2h, b1h)
    b3h = b3.astype(jnp.bfloat16)
    high = COEF[4] * b1 + COEF[5] * b2 + COEF[6] * b3
    rest = COEF[1] * b1 + COEF[2] * b2 + COEF[3] * b3 + dot(b3h, high.astype(jnp.bfloat16))
    return rest.astype(jnp.bfloat16)


def direction_kernel(pieces_ref, stats_ref, out_ref):
    groups, _, rows, width = pieces_ref.shape
    grad = pieces_ref[...].reshape(groups * rows, width)
    left = root_rest(0.5 * stats_ref[0, 0] + 0.5 * dot(grad, grad, ((1,), (1,))))
    right = root_rest(0.5 * stats_ref[0, 1] + 0.5 * dot(grad, grad, ((0,), (0,))))
    wide = grad.astype(jnp.float32)
    half = COEF[0] * wide + dot(left, grad)
    pre = COEF[0] * half + dot(half.astype(jnp.bfloat16), right)
    count = 1.0 / (groups * rows * width)
    grad_mean = jnp.sum(wide * wide, axis=(0, 1), keepdims=True) * count
    pre_mean = jnp.sum(pre * pre, axis=(0, 1), keepdims=True) * count
    result = pre * (jnp.sqrt(grad_mean) / jnp.sqrt(pre_mean + 1e-06))
    out_ref[...] = result.astype(jnp.bfloat16).reshape(groups, 1, rows, width)


def directions(pieces, stats):
    groups, places, rows, width = pieces.shape
    return pl.pallas_call(
        direction_kernel,
        grid=(places,),
        in_specs=[
            pl.BlockSpec((groups, 1, rows, width), lambda k: (0, k, 0, 0)),
            pl.BlockSpec((1, 2, width, width), lambda k: (k, 0, 0, 0)),
        ],
        out_specs=pl.BlockSpec((groups, 1, rows, width), lambda k: (0, k, 0, 0)),
        out_shape=jax.ShapeDtypeStruct(pieces.shape, jnp.bfloat16),
        compiler_params=pltpu.CompilerParams(vmem_limit_bytes=48 * MIB),
    )(pieces, stats)


def pick_kernel(index_ref, in_ref, out_ref):
    for place in range(out_ref.shape[0]):
        out_ref[place] = in_ref[index_ref[place]].astype(out_ref.dtype)


def pick(index, array, dtype):
    return pl.pallas_call(
        pick_kernel,
        in_specs=[
            pl.BlockSpec(memory_space=pltpu.SMEM),
            pl.BlockSpec(memory_space=pltpu.VMEM),
        ],
        out_specs=pl.BlockSpec(memory_space=pltpu.VMEM),
        out_shape=jax.ShapeDtypeStruct(index.shape + array.shape[1:], dtype),
        compiler_params=pltpu.CompilerParams(vmem_limit_bytes=16 * MIB),
    )(index, array)


def send(array, perm):
    return lax.ppermute(array, "dp", perm)


def wide(array):
    return array.astype(jnp.float32)


def coded(array):
    return array.astype(jnp.float16)


def summed_rows(local, count):
    me = lax.axis_index("dp")
    y, z, c = me // (NZ * NC), (me // NC) % NZ, me % NC
    half = count // 2

    def part(dy, dz, dc):
        block = (((y + dy) % NY) * NZ + (z + dz) % NZ) * NC + (c + dc) % NC
        return lax.dynamic_slice_in_dim(local, block * count, count, axis=0)

    def both_cores(dy, dz):
        other = send(part(dy, dz, 1), CORE)
        return (wide(part(dy, dz, 0)) + wide(other)) * SCALE

    def over_y(dz):
        far = both_cores(2, dz)
        up_far = send(coded(far[:half]), UP)
        down_far = send(coded(far[half:]), DOWN)
        above = both_cores(1, dz)
        below = both_cores(3, dz)
        from_below_late = send(coded(above[half:]), UP)
        from_above_early = send(coded(below[:half]), DOWN)
        from_below_early = send(coded(above[:half] + wide(up_far)), UP)
        from_above_late = send(coded(below[half:] + wide(down_far)), DOWN)
        mine = both_cores(0, dz)
        early = mine[:half] + (wide(from_below_early) + wide(from_above_early))
        late = mine[half:] + (wide(from_below_late) + wide(from_above_late))
        return early, late

    early, late = over_y(1)
    other = send(jnp.concatenate([coded(early), coded(late)]), ZHI)
    early, late = over_y(0)
    total = jnp.concatenate([early, late]) + wide(other)
    return (total * (1.0 / SCALE)).astype(jnp.bfloat16)


def body(partial_grads, owners, prev_stats):
    groups = lax.axis_size("grp")
    places = prev_stats.shape[2]
    owner_row = owners[0, :, 0]
    count = owner_row.shape[0]
    blocks = jnp.arange(count, dtype=jnp.int32)
    same = owner_row[:, None] == owner_row[None, :]
    before = blocks[None, :] < blocks[:, None]
    slot = jnp.sum(jnp.where(same & before, 1, 0), axis=1).astype(jnp.int32)
    place = owner_row * places + slot
    every = jnp.arange(groups * places, dtype=jnp.int32)
    held = jnp.sum(jnp.where(place[None, :] == every[:, None], blocks[None, :], 0), axis=1).astype(jnp.int32)

    grad_rows = summed_rows(partial_grads[0], count)
    _, rows, width = grad_rows.shape
    outgoing = pick(held, grad_rows, jnp.bfloat16).reshape(groups, places, rows, width)
    pieces = lax.all_to_all(outgoing, "grp", split_axis=0, concat_axis=0, tiled=True)
    result = directions(pieces, prev_stats[0, 0])
    back = lax.all_to_all(result, "grp", split_axis=0, concat_axis=0, tiled=True)
    return pick(place, back.reshape(groups * places, rows, width), jnp.float32)


def solution(mesh):
    in_specs = (
        P("dp", None, "grp", None),
        P("dp", None, None),
        P("dp", "grp", None, None, None, None),
    )
    out_specs = P("dp", "grp", None)
    return jax.shard_map(body, mesh=mesh, in_specs=in_specs, out_specs=out_specs, check_vma=False)
```

```python
from math import comb

import jax
import jax.numpy as jnp
from jax import lax
from jax.experimental import pallas as pl
from jax.experimental.pallas import tpu as pltpu
from jax.sharding import PartitionSpec as P

NY, NZ, NC = 4, 2, 2
SCALE = 1024.0
MIB = 1024 * 1024


def dp_perm(target):
    pairs = []
    for y in range(NY):
        for z in range(NZ):
            for c in range(NC):
                ty, tz, tc = target(y, z, c)
                pairs.append(((y * NZ + z) * NC + c, (ty * NZ + tz) * NC + tc))
    return pairs


CORE = dp_perm(lambda y, z, c: (y, z, 1 - c))
NEXT = dp_perm(lambda y, z, c: (y ^ 1 if c == 0 else 3 - y, z, c))
LAST = dp_perm(lambda y, z, c: (3 - y if c == 0 else y ^ 1, z, c))
OTHER_Z = dp_perm(lambda y, z, c: (y, 1 - z, c))
OPPOSITE = dp_perm(lambda y, z, c: (y ^ 2, z, c))
NX, NLO = 4, 4


def ring_perm():
    pairs = []
    for dp in range(NY * NZ * NC):
        for grp in range(NX * NLO):
            y, hi, c = dp // (NZ * NC), (dp // NC) % NZ, dp % NC
            x, lo = grp // NLO, grp % NLO
            ring = (hi * NLO + lo + (2 if c == 0 else -2)) % (NZ * NLO)
            target = (y * NZ + ring // NLO) * NC + c
            pairs.append((dp * NX * NLO + grp, target * NX * NLO + x * NLO + ring % NLO))
    return pairs


ALONG_Z = ring_perm()


def root_coefficients():
    f0, f1 = 27.0 / 22.0, -5.0 / 22.0
    fifth = [comb(5, i) * f0 ** (5 - i) * f1**i for i in range(6)]
    product = [0.0] * 7
    for i, value in enumerate(fifth):
        product[i] += value / 11.0
        product[i + 1] += value * 10.0 / 11.0
    coefs = [-value / 4.0 for value in product]
    coefs[0] += 5.0 * f0 / 4.0
    coefs[1] += 5.0 * f1 / 4.0
    return [value * 1.1 ** (-0.25) for value in coefs]


COEF = root_coefficients()


def dot(a, b, dims=((1,), (0,))):
    return lax.dot_general(a, b, (dims, ((), ())), preferred_element_type=jnp.float32)


def gram_kernel(pieces_ref, stats_ref, out_ref, held, arrived):
    groups, places, rows, width = pieces_ref.shape
    size = groups * rows
    slots = range(places)
    chains = [(k, side) for k in slots for side in range(2)]
    copies = [pltpu.make_async_copy(stats_ref.at[k], held.at[k], arrived.at[k]) for k in slots]
    for copy in copies:
        copy.start()
    grads = [pieces_ref[:, k].reshape(size, width) for k in slots]
    grams = [dot(grads[k], grads[k], ((1 - side,), (1 - side,))) for k, side in chains]
    for copy in copies:
        copy.wait()
    sums = [held[k, side] + gram for (k, side), gram in zip(chains, grams)]
    scales = []
    for s in sums:
        mean = jnp.sum(s * s, axis=(0, 1), keepdims=True) * (0.25 / (width * width))
        scales.append(0.5 / (width * jnp.sqrt(mean + 1e-06)))
    b1 = [s * scale for s, scale in zip(sums, scales)]
    b1h = [b.astype(jnp.bfloat16) for b in b1]
    b2 = [dot(b, b) for b in b1h]
    b2h = [b.astype(jnp.bfloat16) for b in b2]
    b3 = [dot(p, q) for p, q in zip(b2h, b1h)]
    b3h = [b.astype(jnp.bfloat16) for b in b3]
    high = [(COEF[4] * p + COEF[5] * q + COEF[6] * r).astype(jnp.bfloat16) for p, q, r in zip(b1, b2, b3)]
    low = [COEF[1] * p + COEF[2] * q + COEF[3] * r for p, q, r in zip(b1, b2, b3)]
    rest = [(l + dot(p, q)).astype(jnp.bfloat16) for l, p, q in zip(low, b3h, high)]
    count = 1.0 / (size * width)
    wides = [grad.astype(jnp.float32) for grad in grads]
    halves = [COEF[0] * wides[k] + dot(rest[2 * k], grads[k]) for k in slots]
    pres = [COEF[0] * halves[k] + dot(halves[k].astype(jnp.bfloat16), rest[2 * k + 1]) for k in slots]
    for k in slots:
        grad_mean = jnp.sum(wides[k] * wides[k], axis=(0, 1), keepdims=True) * count
        pre_mean = jnp.sum(pres[k] * pres[k], axis=(0, 1), keepdims=True) * count
        result = pres[k] * (jnp.sqrt(grad_mean) / jnp.sqrt(pre_mean + 1e-06))
        out_ref[:, k] = result.astype(jnp.bfloat16).reshape(groups, rows, width)


def directions(pieces, stats):
    return pl.pallas_call(
        gram_kernel,
        in_specs=[
            pl.BlockSpec(memory_space=pltpu.VMEM),
            pl.BlockSpec(memory_space=pl.ANY),
        ],
        out_specs=pl.BlockSpec(memory_space=pltpu.VMEM),
        out_shape=jax.ShapeDtypeStruct(pieces.shape, jnp.bfloat16),
        scratch_shapes=[
            pltpu.VMEM(stats.shape, jnp.float32),
            pltpu.SemaphoreType.DMA((stats.shape[0],)),
        ],
        compiler_params=pltpu.CompilerParams(vmem_limit_bytes=48 * MIB),
    )(pieces, stats)


def pick_kernel(index_ref, in_ref, out_ref):
    for place in range(out_ref.shape[0]):
        out_ref[place] = in_ref[index_ref[place]].astype(out_ref.dtype)


def pick(index, array, dtype):
    return pl.pallas_call(
        pick_kernel,
        in_specs=[
            pl.BlockSpec(memory_space=pltpu.SMEM),
            pl.BlockSpec(memory_space=pltpu.VMEM),
        ],
        out_specs=pl.BlockSpec(memory_space=pltpu.VMEM),
        out_shape=jax.ShapeDtypeStruct(index.shape + array.shape[1:], dtype),
        compiler_params=pltpu.CompilerParams(vmem_limit_bytes=16 * MIB),
    )(index, array)


def send(array, perm):
    return lax.ppermute(array, "dp", perm)


def wide(array):
    return array.astype(jnp.float32)


def coded(array):
    return array.astype(jnp.float16)


def after(value, *others):
    return lax.optimization_barrier((value,) + others)[0]


def summed_rows(local, count):
    me = lax.axis_index("dp")
    y, z, c = me // (NZ * NC), (me // NC) % NZ, me % NC
    following = jnp.where(c == 0, y ^ 1, 3 - y)
    preceding = jnp.where(c == 0, 3 - y, y ^ 1)
    opposite = y ^ 2
    _, rows, width = local.shape
    parts = local.reshape(NY, NZ, NC, count, rows, width)

    def held(source, dz, dc):
        at = (0, z ^ dz, c ^ dc, 0, 0, 0)
        return lax.dynamic_slice(source, at, (NY, 1, 1, count, rows, width)).reshape(NY, count, rows, width)

    def part(at_y, dz, other):
        at = (at_y, z ^ dz, c, 0, 0, 0)
        mine = lax.dynamic_slice(parts, at, (1, 1, 1, count, rows, width)).reshape(count, rows, width)
        theirs = lax.dynamic_slice(other, (at_y, 0, 0, 0), (1, count, rows, width)).reshape(count, rows, width)
        return (wide(mine) + wide(theirs)) * SCALE

    to_core1 = held(parts, 1, 1)
    other1 = send(to_core1, CORE)
    other0 = send(held(after(parts, to_core1), 0, 1), CORE)
    first1 = coded(part(opposite, 1, other1)), coded(part(following, 1, other1))
    far1, near1 = (send(value, NEXT) for value in first1)
    second1 = coded(part(preceding, 1, other1) + wide(far1))
    last1 = send(second1, LAST)
    other0 = after(other0, second1)
    direct = [coded(part(at, 0, other0)) for at in (opposite, following, preceding)]
    crossing = coded(part(y, 1, after(other1, *direct)) + (wide(near1) + wide(last1)))
    crossed = send(crossing, OTHER_Z)
    along0 = [send(value, pairs) for value, pairs in zip(direct, (OPPOSITE, NEXT, LAST))]
    other0 = after(other0, crossing, *direct)
    mine = part(y, 0, other0) + (wide(along0[0]) + wide(along0[1]) + wide(along0[2]))
    whole = lax.optimization_barrier(mine)
    return ((whole + wide(crossed)) * (1.0 / SCALE)).astype(jnp.bfloat16)


def body(partial_grads, owners, prev_stats):
    groups = lax.axis_size("grp")
    places = prev_stats.shape[2]
    owner_row = owners[0, :, 0]
    count = owner_row.shape[0]
    blocks = jnp.arange(count, dtype=jnp.int32)
    same = owner_row[:, None] == owner_row[None, :]
    before = blocks[None, :] < blocks[:, None]
    slot = jnp.sum(jnp.where(same & before, 1, 0), axis=1).astype(jnp.int32)
    place = owner_row * places + slot
    every = jnp.arange(groups * places, dtype=jnp.int32)
    held = jnp.sum(jnp.where(place[None, :] == every[:, None], blocks[None, :], 0), axis=1).astype(jnp.int32)

    grad_rows = summed_rows(partial_grads[0], count)
    _, rows, width = grad_rows.shape
    outgoing = pick(held, grad_rows, jnp.bfloat16).reshape(groups, places, rows, width)
    pieces = lax.all_to_all(outgoing, "grp", split_axis=0, concat_axis=0, tiled=True)
    result = directions(pieces, prev_stats[0, 0])
    back = lax.all_to_all(result, "grp", split_axis=0, concat_axis=0, tiled=True)
    return pick(place, back.reshape(groups * places, rows, width), jnp.float32)


def solution(mesh):
    in_specs = (
        P("dp", None, "grp", None),
        P("dp", None, None),
        P("dp", "grp", None, None, None, None),
    )
    out_specs = P("dp", "grp", None)
    return jax.shard_map(body, mesh=mesh, in_specs=in_specs, out_specs=out_specs, check_vma=False)
```

```python
from math import comb

import jax
import jax.numpy as jnp
from jax import lax
from jax.experimental import pallas as pl
from jax.experimental.pallas import tpu as pltpu
from jax.sharding import PartitionSpec as P

NY, NZ, NC = 4, 2, 2
SCALE = 1024.0
MIB = 1024 * 1024


def dp_perm(target):
    pairs = []
    for y in range(NY):
        for z in range(NZ):
            for c in range(NC):
                ty, tz, tc = target(y, z, c)
                pairs.append(((y * NZ + z) * NC + c, (ty * NZ + tz) * NC + tc))
    return pairs


CORE = dp_perm(lambda y, z, c: (y, z, 1 - c))
NEXT = dp_perm(lambda y, z, c: (y ^ 1 if c == 0 else 3 - y, z, c))
LAST = dp_perm(lambda y, z, c: (3 - y if c == 0 else y ^ 1, z, c))
OTHER_Z = dp_perm(lambda y, z, c: (y, 1 - z, c))
OPPOSITE = dp_perm(lambda y, z, c: (y ^ 2, z, c))

def root_coefficients():
    f0, f1 = 27.0 / 22.0, -5.0 / 22.0
    fifth = [comb(5, i) * f0 ** (5 - i) * f1**i for i in range(6)]
    product = [0.0] * 7
    for i, value in enumerate(fifth):
        product[i] += value / 11.0
        product[i + 1] += value * 10.0 / 11.0
    coefs = [-value / 4.0 for value in product]
    coefs[0] += 5.0 * f0 / 4.0
    coefs[1] += 5.0 * f1 / 4.0
    return [value * 1.1 ** (-0.25) for value in coefs]


COEF = root_coefficients()


def dot(a, b, dims=((1,), (0,))):
    return lax.dot_general(a, b, (dims, ((), ())), preferred_element_type=jnp.float32)


def gram_kernel(pieces_ref, stats_ref, out_ref, held, arrived):
    groups, places, rows, width = pieces_ref.shape
    size = groups * rows
    slots = range(places)
    chains = [(k, side) for k in slots for side in range(2)]
    copies = [pltpu.make_async_copy(stats_ref.at[k], held.at[k], arrived.at[k]) for k in slots]
    for copy in copies:
        copy.start()
    grads = [pieces_ref[:, k].reshape(size, width) for k in slots]
    grams = [dot(grads[k], grads[k], ((1 - side,), (1 - side,))) for k, side in chains]
    for copy in copies:
        copy.wait()
    sums = [held[k, side] + gram for (k, side), gram in zip(chains, grams)]
    scales = []
    for s in sums:
        mean = jnp.sum(s * s, axis=(0, 1), keepdims=True) * (0.25 / (width * width))
        scales.append(0.5 / (width * jnp.sqrt(mean + 1e-06)))
    b1 = [s * scale for s, scale in zip(sums, scales)]
    b1h = [b.astype(jnp.bfloat16) for b in b1]
    b2 = [dot(b, b) for b in b1h]
    b2h = [b.astype(jnp.bfloat16) for b in b2]
    b3 = [dot(p, q) for p, q in zip(b2h, b1h)]
    b3h = [b.astype(jnp.bfloat16) for b in b3]
    high = [(COEF[4] * p + COEF[5] * q + COEF[6] * r).astype(jnp.bfloat16) for p, q, r in zip(b1, b2, b3)]
    low = [COEF[1] * p + COEF[2] * q + COEF[3] * r for p, q, r in zip(b1, b2, b3)]
    rest = [(l + dot(p, q)).astype(jnp.bfloat16) for l, p, q in zip(low, b3h, high)]
    count = 1.0 / (size * width)
    wides = [grad.astype(jnp.float32) for grad in grads]
    halves = [COEF[0] * wides[k] + dot(rest[2 * k], grads[k]) for k in slots]
    pres = [COEF[0] * halves[k] + dot(halves[k].astype(jnp.bfloat16), rest[2 * k + 1]) for k in slots]
    for k in slots:
        grad_mean = jnp.sum(wides[k] * wides[k], axis=(0, 1), keepdims=True) * count
        pre_mean = jnp.sum(pres[k] * pres[k], axis=(0, 1), keepdims=True) * count
        result = pres[k] * (jnp.sqrt(grad_mean) / jnp.sqrt(pre_mean + 1e-06))
        out_ref[:, k] = result.astype(jnp.bfloat16).reshape(groups, rows, width)


def directions(pieces, stats):
    return pl.pallas_call(
        gram_kernel,
        in_specs=[
            pl.BlockSpec(memory_space=pltpu.VMEM),
            pl.BlockSpec(memory_space=pl.ANY),
        ],
        out_specs=pl.BlockSpec(memory_space=pltpu.VMEM),
        out_shape=jax.ShapeDtypeStruct(pieces.shape, jnp.bfloat16),
        scratch_shapes=[
            pltpu.VMEM(stats.shape, jnp.float32),
            pltpu.SemaphoreType.DMA((stats.shape[0],)),
        ],
        compiler_params=pltpu.CompilerParams(vmem_limit_bytes=48 * MIB),
    )(pieces, stats)


def pick_kernel(index_ref, in_ref, out_ref):
    for place in range(out_ref.shape[0]):
        out_ref[place] = in_ref[index_ref[place]].astype(out_ref.dtype)


def pick(index, array, dtype):
    return pl.pallas_call(
        pick_kernel,
        in_specs=[
            pl.BlockSpec(memory_space=pltpu.SMEM),
            pl.BlockSpec(memory_space=pltpu.VMEM),
        ],
        out_specs=pl.BlockSpec(memory_space=pltpu.VMEM),
        out_shape=jax.ShapeDtypeStruct(index.shape + array.shape[1:], dtype),
        compiler_params=pltpu.CompilerParams(vmem_limit_bytes=16 * MIB),
    )(index, array)


def send(array, perm):
    return lax.ppermute(array, "dp", perm)


def wide(array):
    return array.astype(jnp.float32)


def coded(array):
    return array.astype(jnp.float16)


def after(value, *others):
    return lax.optimization_barrier((value,) + others)[0]


def summed_rows(local, count):
    me = lax.axis_index("dp")
    y, z, c = me // (NZ * NC), (me // NC) % NZ, me % NC
    following = jnp.where(c == 0, y ^ 1, 3 - y)
    preceding = jnp.where(c == 0, 3 - y, y ^ 1)
    opposite = y ^ 2
    _, rows, width = local.shape
    parts = local.reshape(NY, NZ, NC, count, rows, width)

    def held(source, dz, dc):
        at = (0, z ^ dz, c ^ dc, 0, 0, 0)
        return lax.dynamic_slice(source, at, (NY, 1, 1, count, rows, width)).reshape(NY, count, rows, width)

    def part(at_y, dz, other):
        at = (at_y, z ^ dz, c, 0, 0, 0)
        mine = lax.dynamic_slice(parts, at, (1, 1, 1, count, rows, width)).reshape(count, rows, width)
        theirs = lax.dynamic_slice(other, (at_y, 0, 0, 0), (1, count, rows, width)).reshape(count, rows, width)
        return (wide(mine) + wide(theirs)) * SCALE

    def wanted(source, at_y):
        at = (at_y, z ^ 1, c ^ 1, 0, 0, 0)
        return lax.dynamic_slice(source, at, (1, 1, 1, count, rows, width)).reshape(1, count, rows, width)

    def joined(at_y, other):
        at = (at_y, z ^ 1, c, 0, 0, 0)
        mine = lax.dynamic_slice(parts, at, (1, 1, 1, count, rows, width)).reshape(count, rows, width)
        return (wide(mine) + wide(other[0])) * SCALE

    early = wanted(parts, opposite), wanted(parts, preceding)
    early1 = [send(value, CORE) for value in early]
    source = after(parts, *early)
    late = wanted(source, following), wanted(source, y)
    late1 = [send(value, CORE) for value in late]
    first1 = coded(joined(opposite, early1[0])), coded(joined(following, early1[1]))
    far1, near1 = (send(value, NEXT) for value in first1)
    to_core0 = held(after(parts, *late, *first1), 0, 1)
    other0 = send(to_core0, CORE)
    direct = [coded(part(opposite, 0, other0))]
    second1 = coded(joined(preceding, after(late1[0], *direct)) + wide(far1))
    last1 = send(second1, LAST)
    other0 = after(other0, second1)
    direct += [coded(part(at, 0, other0)) for at in (following, preceding)]
    crossing = coded(joined(y, after(late1[1], *direct)) + (wide(near1) + wide(last1)))
    crossed = send(crossing, OTHER_Z)
    along0 = [send(value, pairs) for value, pairs in zip(direct, (OPPOSITE, NEXT, LAST))]
    other0 = after(other0, crossing, *direct)
    mine = part(y, 0, other0) + (wide(along0[0]) + wide(along0[1]) + wide(along0[2]))
    whole = lax.optimization_barrier(mine)
    return ((whole + wide(crossed)) * (1.0 / SCALE)).astype(jnp.bfloat16)


def body(partial_grads, owners, prev_stats):
    groups = lax.axis_size("grp")
    places = prev_stats.shape[2]
    owner_row = owners[0, :, 0]
    count = owner_row.shape[0]
    blocks = jnp.arange(count, dtype=jnp.int32)
    same = owner_row[:, None] == owner_row[None, :]
    before = blocks[None, :] < blocks[:, None]
    slot = jnp.sum(jnp.where(same & before, 1, 0), axis=1).astype(jnp.int32)
    place = owner_row * places + slot
    every = jnp.arange(groups * places, dtype=jnp.int32)
    held = jnp.sum(jnp.where(place[None, :] == every[:, None], blocks[None, :], 0), axis=1).astype(jnp.int32)

    grad_rows = summed_rows(partial_grads[0], count)
    _, rows, width = grad_rows.shape
    outgoing = pick(held, grad_rows, jnp.bfloat16).reshape(groups, places, rows, width)
    pieces = lax.all_to_all(outgoing, "grp", split_axis=0, concat_axis=0, tiled=True)
    result = directions(pieces, prev_stats[0, 0])
    back = lax.all_to_all(result, "grp", split_axis=0, concat_axis=0, tiled=True)
    return pick(place, back.reshape(groups * places, rows, width), jnp.float32)


def solution(mesh):
    in_specs = (
        P("dp", None, "grp", None),
        P("dp", None, None),
        P("dp", "grp", None, None, None, None),
    )
    out_specs = P("dp", "grp", None)
    return jax.shard_map(body, mesh=mesh, in_specs=in_specs, out_specs=out_specs, check_vma=False)
```

```python
from math import comb

import jax
import jax.numpy as jnp
from jax import lax
from jax.experimental import pallas as pl
from jax.experimental.pallas import tpu as pltpu
from jax.sharding import PartitionSpec as P

NY, NZ, NC = 4, 2, 2
SCALE = 1024.0
MIB = 1024 * 1024


def dp_perm(target):
    pairs = []
    for y in range(NY):
        for z in range(NZ):
            for c in range(NC):
                ty, tz, tc = target(y, z, c)
                pairs.append(((y * NZ + z) * NC + c, (ty * NZ + tz) * NC + tc))
    return pairs


CORE = dp_perm(lambda y, z, c: (y, z, 1 - c))
NEXT = dp_perm(lambda y, z, c: (y ^ 1 if c == 0 else 3 - y, z, c))
LAST = dp_perm(lambda y, z, c: (3 - y if c == 0 else y ^ 1, z, c))
OTHER_Z = dp_perm(lambda y, z, c: (y, 1 - z, c))
OPPOSITE = dp_perm(lambda y, z, c: (y ^ 2, z, c))

def root_coefficients():
    f0, f1 = 27.0 / 22.0, -5.0 / 22.0
    fifth = [comb(5, i) * f0 ** (5 - i) * f1**i for i in range(6)]
    product = [0.0] * 7
    for i, value in enumerate(fifth):
        product[i] += value / 11.0
        product[i + 1] += value * 10.0 / 11.0
    coefs = [-value / 4.0 for value in product]
    coefs[0] += 5.0 * f0 / 4.0
    coefs[1] += 5.0 * f1 / 4.0
    return [value * 1.1 ** (-0.25) for value in coefs]


COEF = root_coefficients()


def dot(a, b, dims=((1,), (0,))):
    return lax.dot_general(a, b, (dims, ((), ())), preferred_element_type=jnp.float32)


def gram_kernel(pieces_ref, stats_ref, out_ref, held, arrived):
    groups, places, rows, width = pieces_ref.shape
    size = groups * rows
    slots = range(places)
    chains = [(k, side) for k in slots for side in range(2)]
    copies = [pltpu.make_async_copy(stats_ref.at[k], held.at[k], arrived.at[k]) for k in slots]
    for copy in copies:
        copy.start()
    grads = [pieces_ref[:, k].reshape(size, width) for k in slots]
    grams = [dot(grads[k], grads[k], ((1 - side,), (1 - side,))) for k, side in chains]
    for copy in copies:
        copy.wait()
    sums = [held[k, side] + gram for (k, side), gram in zip(chains, grams)]
    scales = []
    for s in sums:
        mean = jnp.sum(s * s, axis=(0, 1), keepdims=True) * (0.25 / (width * width))
        scales.append(0.5 / (width * jnp.sqrt(mean + 1e-06)))
    b1 = [s * scale for s, scale in zip(sums, scales)]
    b1h = [b.astype(jnp.bfloat16) for b in b1]
    b2 = [dot(b, b) for b in b1h]
    b2h = [b.astype(jnp.bfloat16) for b in b2]
    b3 = [dot(p, q) for p, q in zip(b2h, b1h)]
    b3h = [b.astype(jnp.bfloat16) for b in b3]
    high = [(COEF[4] * p + COEF[5] * q + COEF[6] * r).astype(jnp.bfloat16) for p, q, r in zip(b1, b2, b3)]
    low = [COEF[1] * p + COEF[2] * q + COEF[3] * r for p, q, r in zip(b1, b2, b3)]
    rest = [(l + dot(p, q)).astype(jnp.bfloat16) for l, p, q in zip(low, b3h, high)]
    count = 1.0 / (size * width)
    wides = [grad.astype(jnp.float32) for grad in grads]
    halves = [COEF[0] * wides[k] + dot(rest[2 * k], grads[k]) for k in slots]
    pres = [COEF[0] * halves[k] + dot(halves[k].astype(jnp.bfloat16), rest[2 * k + 1]) for k in slots]
    for k in slots:
        grad_mean = jnp.sum(wides[k] * wides[k], axis=(0, 1), keepdims=True) * count
        pre_mean = jnp.sum(pres[k] * pres[k], axis=(0, 1), keepdims=True) * count
        result = pres[k] * (jnp.sqrt(grad_mean) / jnp.sqrt(pre_mean + 1e-06))
        out_ref[:, k] = result.astype(jnp.bfloat16).reshape(groups, rows, width)


def directions(pieces, stats):
    return pl.pallas_call(
        gram_kernel,
        in_specs=[
            pl.BlockSpec(memory_space=pltpu.VMEM),
            pl.BlockSpec(memory_space=pl.ANY),
        ],
        out_specs=pl.BlockSpec(memory_space=pltpu.VMEM),
        out_shape=jax.ShapeDtypeStruct(pieces.shape, jnp.bfloat16),
        scratch_shapes=[
            pltpu.VMEM(stats.shape, jnp.float32),
            pltpu.SemaphoreType.DMA((stats.shape[0],)),
        ],
        compiler_params=pltpu.CompilerParams(vmem_limit_bytes=48 * MIB),
    )(pieces, stats)


def pick_kernel(index_ref, in_ref, out_ref):
    for place in range(out_ref.shape[0]):
        out_ref[place] = in_ref[index_ref[place]].astype(out_ref.dtype)


def pick(index, array, dtype):
    return pl.pallas_call(
        pick_kernel,
        in_specs=[
            pl.BlockSpec(memory_space=pltpu.SMEM),
            pl.BlockSpec(memory_space=pltpu.VMEM),
        ],
        out_specs=pl.BlockSpec(memory_space=pltpu.VMEM),
        out_shape=jax.ShapeDtypeStruct(index.shape + array.shape[1:], dtype),
        compiler_params=pltpu.CompilerParams(vmem_limit_bytes=16 * MIB),
    )(index, array)


def fetch_kernel(index_ref, in_ref, out_ref, taken, widened, arrived, written):
    count = out_ref.shape[0]
    loads = [pltpu.make_async_copy(in_ref.at[index_ref[k]], taken.at[k], arrived.at[k]) for k in range(count)]
    stores = [pltpu.make_async_copy(widened.at[k], out_ref.at[k], written.at[k]) for k in range(count)]
    for load in loads:
        load.start()
    for k in range(count):
        loads[k].wait()
        widened[k] = taken[k].astype(widened.dtype)
        stores[k].start()
    for store in stores:
        store.wait()


def fetch(index, array, dtype):
    count, block = index.shape[0], array.shape[1:]
    return pl.pallas_call(
        fetch_kernel,
        in_specs=[
            pl.BlockSpec(memory_space=pltpu.SMEM),
            pl.BlockSpec(memory_space=pl.ANY),
        ],
        out_specs=pl.BlockSpec(memory_space=pl.ANY),
        out_shape=jax.ShapeDtypeStruct((count,) + block, dtype),
        scratch_shapes=[
            pltpu.VMEM((count,) + block, array.dtype),
            pltpu.VMEM((count,) + block, dtype),
            pltpu.SemaphoreType.DMA((count,)),
            pltpu.SemaphoreType.DMA((count,)),
        ],
        compiler_params=pltpu.CompilerParams(vmem_limit_bytes=16 * MIB),
    )(index, array)


def send(array, perm):
    return lax.ppermute(array, "dp", perm)


def wide(array):
    return array.astype(jnp.float32)


def coded(array):
    return array.astype(jnp.float16)


def after(value, *others):
    return lax.optimization_barrier((value,) + others)[0]


def summed_rows(local, count):
    me = lax.axis_index("dp")
    y, z, c = me // (NZ * NC), (me // NC) % NZ, me % NC
    following = jnp.where(c == 0, y ^ 1, 3 - y)
    preceding = jnp.where(c == 0, 3 - y, y ^ 1)
    opposite = y ^ 2
    _, rows, width = local.shape
    parts = local.reshape(NY, NZ, NC, count, rows, width)

    def held(source, dz, dc):
        at = (0, z ^ dz, c ^ dc, 0, 0, 0)
        return lax.dynamic_slice(source, at, (NY, 1, 1, count, rows, width)).reshape(NY, count, rows, width)

    def part(at_y, dz, other):
        at = (at_y, z ^ dz, c, 0, 0, 0)
        mine = lax.dynamic_slice(parts, at, (1, 1, 1, count, rows, width)).reshape(count, rows, width)
        theirs = lax.dynamic_slice(other, (at_y, 0, 0, 0), (1, count, rows, width)).reshape(count, rows, width)
        return (wide(mine) + wide(theirs)) * SCALE

    def wanted(source, at_y):
        at = (at_y, z ^ 1, c ^ 1, 0, 0, 0)
        return lax.dynamic_slice(source, at, (1, 1, 1, count, rows, width)).reshape(1, count, rows, width)

    def joined(at_y, other):
        at = (at_y, z ^ 1, c, 0, 0, 0)
        mine = lax.dynamic_slice(parts, at, (1, 1, 1, count, rows, width)).reshape(count, rows, width)
        return (wide(mine) + wide(other[0])) * SCALE

    early = wanted(parts, opposite), wanted(parts, preceding)
    early1 = [send(value, CORE) for value in early]
    source = after(parts, *early)
    late = wanted(source, following), wanted(source, y)
    late1 = [send(value, CORE) for value in late]
    first1 = coded(joined(opposite, early1[0])), coded(joined(following, early1[1]))
    far1, near1 = (send(value, NEXT) for value in first1)
    to_core0 = held(after(parts, *late, *first1), 0, 1)
    other0 = send(to_core0, CORE)
    direct = [coded(part(opposite, 0, other0))]
    second1 = coded(joined(preceding, after(late1[0], *direct)) + wide(far1))
    last1 = send(second1, LAST)
    other0 = after(other0, second1)
    direct += [coded(part(at, 0, other0)) for at in (following, preceding)]
    crossing = coded(joined(y, after(late1[1], *direct)) + (wide(near1) + wide(last1)))
    crossed = send(crossing, OTHER_Z)
    along0 = [send(value, pairs) for value, pairs in zip(direct, (OPPOSITE, NEXT, LAST))]
    other0 = after(other0, crossing, *direct)
    mine = part(y, 0, other0) + (wide(along0[0]) + wide(along0[1]) + wide(along0[2]))
    whole = lax.optimization_barrier(mine)
    return ((whole + wide(crossed)) * (1.0 / SCALE)).astype(jnp.bfloat16)


def body(partial_grads, owners, prev_stats):
    groups = lax.axis_size("grp")
    places = prev_stats.shape[2]
    owner_row = owners[0, :, 0]
    count = owner_row.shape[0]
    blocks = jnp.arange(count, dtype=jnp.int32)
    same = owner_row[:, None] == owner_row[None, :]
    before = blocks[None, :] < blocks[:, None]
    slot = jnp.sum(jnp.where(same & before, 1, 0), axis=1).astype(jnp.int32)
    place = owner_row * places + slot
    every = jnp.arange(groups * places, dtype=jnp.int32)
    held = jnp.sum(jnp.where(place[None, :] == every[:, None], blocks[None, :], 0), axis=1).astype(jnp.int32)

    grad_rows = summed_rows(partial_grads[0], count)
    _, rows, width = grad_rows.shape
    outgoing = pick(held, grad_rows, jnp.bfloat16).reshape(groups, places, rows, width)
    pieces = lax.all_to_all(outgoing, "grp", split_axis=0, concat_axis=0, tiled=True)
    result = directions(pieces, prev_stats[0, 0])
    back = lax.all_to_all(result, "grp", split_axis=0, concat_axis=0, tiled=True)
    return fetch(place, back.reshape(groups * places, rows, width), jnp.float32)


def solution(mesh):
    in_specs = (
        P("dp", None, "grp", None),
        P("dp", None, None),
        P("dp", "grp", None, None, None, None),
    )
    out_specs = P("dp", "grp", None)
    return jax.shard_map(body, mesh=mesh, in_specs=in_specs, out_specs=out_specs, check_vma=False)
```
